32 devices in a mesh: strat: 4 (over y, core), grp: 8 (over z, x).
Axes of the slice: x: 2, y: 2, z: 4, core: 2. Of those that a mesh axis runs over, the one named last changes fastest.
Arguments:
- user_factors: float32 [32768, 256], P(('strat', 'grp')), may hold values from -1.5 to 1.5
- item_factors: float32 [16384, 256], P('strat'), may hold values from -1.5 to 1.5
- tile_coords: int32 [4, 8, 3, 2, 16], P('strat', 'grp'), may hold values from 0 to 31, as said below
- tile_counts: int32 [4, 8, 3], P('strat', 'grp'), may hold values from 5 to 16, as said below
- tile_values: bfloat16 [4, 8, 3, 16, 128, 128], P('strat', 'grp'), may hold values from 0 to 10
Outputs:
- users_out: float32 [32768, 256], P(('strat', 'grp'))
- items_out: float32 [16384, 256], P('strat')
The draws below stay inside these ranges and needn't reach their ends.
Inputs may be any that keep to these rules, and one draw needn't show every extreme that they name: `tile_coords`: each list names distinct tiles; user tiles lie below 8 and item tiles below 32; entries at and after the count are ignored. `tile_counts`: in every sub-epoch some device has exactly 16 live tiles.
All inputs are finite; a program needn't handle non-finite values.
Results may differ from the reference program's by a relative error of at most 0.0018.
Values sent between devices are 32-bit elements; how exact they have to be, the bound alone decides.
No kernel may reach another device: no remote copies, remote signals or barrier semaphores. Data moves between devices by JAX's collectives and lax.ppermute only.
A program may use at most 64 MiB of HBM per device.

```python
import jax
import jax.numpy as jnp
from jax import lax

RANK = 256
TILE = 128
USERS_DEV = 1024
SLAB_ITEMS = 4096
TILES_MAX = 16
SUBEPOCHS = 3
STRATA = 4
MEMBERS = 8


def draw_tile_coords(key, part):
    user_tiles = USERS_DEV // TILE
    item_tiles = SLAB_ITEMS // TILE
    keys = jax.random.split(jax.random.fold_in(key, 11), STRATA * MEMBERS * SUBEPOCHS)
    picks = jax.vmap(lambda k: jax.random.permutation(k, user_tiles * item_tiles)[:TILES_MAX])(keys)
    picks = picks.astype(jnp.int32)
    pairs = jnp.stack([picks // item_tiles, picks % item_tiles], axis=1)
    return pairs.reshape(STRATA, MEMBERS, SUBEPOCHS, 2, TILES_MAX).astype(jnp.int32)


def draw_tile_counts(key, part):
    low = max(1, TILES_MAX // 3)
    base = jax.random.randint(jax.random.fold_in(key, 21), (STRATA * MEMBERS, SUBEPOCHS), low, TILES_MAX + 1).astype(jnp.int32)
    busiest = jax.random.randint(jax.random.fold_in(key, 22), (SUBEPOCHS,), 0, STRATA * MEMBERS).astype(jnp.int32)
    base = base.at[busiest, jnp.arange(SUBEPOCHS)].set(TILES_MAX)
    return base.reshape(STRATA, MEMBERS, SUBEPOCHS).astype(jnp.int32)


def draw_tile_values(key, part):
    shape = (STRATA, MEMBERS, SUBEPOCHS, TILES_MAX, TILE, TILE)
    seen = jax.random.uniform(jax.random.fold_in(key, 31), shape, jnp.float32)
    level = jax.random.uniform(jax.random.fold_in(key, 32), shape, jnp.float32)
    values = jnp.where(seen < 0.4, jnp.exp(level * jnp.log(4.0)), 0.0)
    return values.astype(jnp.bfloat16)


def block_scale(stream_key, extent, pieces, smallest, top_value):
    def one(dim, parts):
        draws = jax.random.uniform(jax.random.fold_in(jax.random.fold_in(stream_key, 6), dim), (parts,), jnp.float32, smallest / len(pieces), top_value / len(pieces))
        return jnp.repeat(jnp.exp(draws), extent[dim] // parts).reshape((-1,) + (1,) * (len(extent) - dim - 1))

    factor_of = one(*pieces[0])
    for cut in pieces[1:]:
        factor_of = factor_of * one(*cut)
    return factor_of


def scatter_about(key, extent, spread, bound, shards=(), kind=jnp.bfloat16):
    gain = block_scale(key, extent, shards, -0.22, 0.18) if shards else 1.0
    drawn = jax.random.normal(key, extent, jnp.float32) * spread * gain
    return jnp.minimum(jnp.maximum(drawn, -bound), bound).astype(kind)


def setup_inputs(seed: int = 0) -> dict:
    seeds = jax.random.split(jax.random.key(seed), 6)
    return {
        "user_factors": scatter_about(seeds[0], (STRATA * MEMBERS * USERS_DEV, RANK), 0.25, 1.5, ((0, 32),), jnp.float32),
        "item_factors": scatter_about(seeds[1], (STRATA * SLAB_ITEMS, RANK), 0.25, 1.5, ((0, 4),), jnp.float32),
        "tile_coords": draw_tile_coords(jax.random.fold_in(seeds[5], 71), 0),
        "tile_counts": draw_tile_counts(jax.random.fold_in(seeds[5], 71), 0),
        "tile_values": draw_tile_values(jax.random.fold_in(seeds[5], 71), 0),
    }


def tile_terms(users_blk, slab, coords, count, values):
    high = lax.Precision.HIGHEST
    user_b = users_blk.astype(jnp.bfloat16).astype(jnp.float32)
    slab_b = slab.astype(jnp.bfloat16).astype(jnp.float32)
    user_tiles = user_b.shape[0] // TILE
    item_tiles = slab_b.shape[0] // TILE
    urows = jnp.take(user_b.reshape(user_tiles, TILE, RANK), coords[0], axis=0)
    irows = jnp.take(slab_b.reshape(item_tiles, TILE, RANK), coords[1], axis=0)
    predicted = jnp.einsum("nrk,nck->nrc", urows, irows, precision=high)
    resid = lax.optimization_barrier((values.astype(jnp.float32) - predicted).astype(jnp.bfloat16))
    resid = resid.astype(jnp.float32)
    user_part = jnp.einsum("nrc,nck->nrk", resid, irows, precision=high)
    item_part = jnp.einsum("nrc,nrk->nck", resid, urows, precision=high)
    live = jnp.arange(coords.shape[1]) < count
    one_user = ((coords[0][:, None] == jnp.arange(user_tiles)[None, :]) & live[:, None]).astype(jnp.float32)
    one_item = ((coords[1][:, None] == jnp.arange(item_tiles)[None, :]) & live[:, None]).astype(jnp.float32)
    user_grad = jnp.einsum("nt,nrk->trk", one_user, user_part, precision=high).reshape(-1, RANK)
    item_grad = jnp.einsum("nt,nrk->trk", one_item, item_part, precision=high).reshape(-1, RANK)
    return user_grad, item_grad


def reference(user_factors, item_factors, tile_coords, tile_counts, tile_values):
    users = user_factors.reshape(STRATA, MEMBERS, USERS_DEV, RANK)
    held = item_factors.reshape(STRATA, SLAB_ITEMS, RANK)
    for sub in range(SUBEPOCHS):
        def one_stratum(pack):
            block, slab, coords, counts, values = pack
            grads_u, grads_i = jax.vmap(lambda u, c, n, v: tile_terms(u, slab, c, n, v))(block, coords, counts, values)
            return grads_u, jnp.sum(grads_i, axis=0)
        user_grad, item_grad = lax.map(one_stratum, (users, held, tile_coords[:, :, sub], tile_counts[:, :, sub], tile_values[:, :, sub]))
        users = users - 0.003 * (0.05 * users - user_grad)
        held = held - 0.003 * (0.05 * held - item_grad)
        if sub + 1 < SUBEPOCHS:
            held = jnp.roll(held, -1, axis=0)
    return users.reshape(-1, RANK), held.reshape(-1, RANK)
```

```python
import functools

import jax
import jax.numpy as jnp
from jax import lax
from jax.experimental import pallas as pl
from jax.experimental.pallas import tpu as pltpu
from jax.sharding import PartitionSpec as P

RATE = 0.003
KEEP = 1.0 - 0.003 * 0.05
WAVES = 2
ANY = pl.BlockSpec(memory_space=pl.ANY)
VMEM = pl.BlockSpec(memory_space=pltpu.VMEM)
SMEM = pl.BlockSpec(memory_space=pltpu.SMEM)


def tile_kernel(sub, wave, side, n_own, *refs):
    fresh = sub == 0
    n_v = 1 if fresh else 2 * n_own
    coords, counts, place, users, running = refs[:5]
    slabs = refs[5 : 5 + n_v]
    values, out_u, near_f, near_b, far, own, held, grad, seen, mine, sems = refs[5 + n_v :]

    copies = []

    def copy(src, dst):
        c = pltpu.make_async_copy(src, dst, sems.at[len(copies)])
        c.start()
        copies.append(c)

    copy(values.at[sub], seen)
    if fresh:
        for way in range(2):
            copy(
                slabs[0].at[:, 2 * wave + way],
                held.at[pl.ds(way * n_own, n_own)],
            )
    else:
        for i, tile in enumerate(slabs):
            copy(tile, held.at[i])
    grad[...] = jnp.zeros_like(grad)
    if wave == 0:
        out_u[...] = users[...] * KEEP
    else:
        out_u[...] = running[...]
    for c in copies:
        c.wait()

    here = place[0]
    count = counts[sub]

    def one(n, carry):
        a = coords[sub, 0, n]
        b = coords[sub, 1, n]

        @pl.when((n < count) & (((b >> 1) & 1) == wave))
        def _():
            owner = b >> 2
            way = b & 1
            ahead = jnp.where(way == 0, here - owner, owner - here)
            slot = way * n_own + lax.rem(ahead + n_own, n_own)
            source = way * n_own + owner if fresh else slot
            rows = pl.ds(pl.multiple_of(a * side, side), side)
            ua = users[rows, :].astype(jnp.bfloat16)
            vb = held[source].astype(jnp.bfloat16)
            guess = lax.dot_general(
                ua, vb, (((1,), (1,)), ((), ())), preferred_element_type=jnp.float32
            )
            resid = (seen[n].astype(jnp.float32) - guess).astype(jnp.bfloat16)
            up = jnp.dot(resid, vb, preferred_element_type=jnp.float32)
            out_u[rows, :] += RATE * up
            ip = lax.dot_general(
                resid, ua, (((0,), (0,)), ((), ())), preferred_element_type=jnp.float32
            )
            grad[slot] += RATE * ip

        return carry

    lax.fori_loop(0, coords.shape[2], one, 0)

    copies.clear()
    copy(grad.at[1], near_f)
    copy(grad.at[n_own + 1], near_b)
    for way in range(2):
        copy(grad.at[pl.ds(way * n_own + 2, n_own - 2)], far.at[way])
    for way in range(2):
        source = way * n_own + here if fresh else way * n_own
        mine[way] = held[source] * KEEP + grad[way * n_own]
    copy(mine, own)
    for c in copies:
        c.wait()


def tile_step(sub, wave, n_own, coords, counts, place, users, running, slabs, values):
    side = values.shape[-1]
    width = users.shape[1]
    tile = jax.ShapeDtypeStruct((side, width), jnp.float32)
    slots = 2 * n_own
    return pl.pallas_call(
        functools.partial(tile_kernel, sub, wave, side, n_own),
        out_shape=(
            jax.ShapeDtypeStruct(users.shape, jnp.float32),
            tile,
            tile,
            jax.ShapeDtypeStruct((2, n_own - 2, side, width), jnp.float32),
            jax.ShapeDtypeStruct((2, side, width), jnp.float32),
        ),
        in_specs=[SMEM, SMEM, SMEM, VMEM, VMEM] + [ANY] * len(slabs) + [ANY],
        out_specs=(VMEM, ANY, ANY, ANY, ANY),
        scratch_shapes=[
            pltpu.VMEM((slots, side, width), jnp.float32),
            pltpu.VMEM((slots, side, width), jnp.float32),
            pltpu.VMEM(values.shape[1:], values.dtype),
            pltpu.VMEM((2, side, width), jnp.float32),
            pltpu.SemaphoreType.DMA((slots + 1,)),
        ],
        compiler_params=pltpu.CompilerParams(vmem_limit_bytes=24 * 2**20),
        cost_estimate=pl.CostEstimate(
            flops=8 * 3 * 2 * side * side * width,
            bytes_accessed=8 * 2**20,
            transcendentals=0,
        ),
        name=f"tiles_{sub}_{wave}",
    )(coords, counts, place, users, running, *slabs, values)


def lay_kernel(wave, n_own, carried, *refs):
    place = refs[0]
    tiles = refs[1 + carried : 1 + carried + 2 * n_own]
    out, sems = refs[1 + carried + 2 * n_own :]
    here = place[0]
    copies = []
    for way in range(2):
        for t in range(n_own):
            owner = lax.rem(here + (n_own - t if way == 0 else t), n_own)
            i = way * n_own + t
            c = pltpu.make_async_copy(tiles[i], out.at[owner, 2 * wave + way], sems.at[i])
            c.start()
            copies.append(c)
    for c in copies:
        c.wait()


def lay(wave, n_own, place, tiles, base):
    side, width = tiles[0].shape
    carried = () if base is None else (base,)
    return pl.pallas_call(
        functools.partial(lay_kernel, wave, n_own, len(carried)),
        out_shape=jax.ShapeDtypeStruct((n_own, 2 * WAVES, side, width), jnp.float32),
        in_specs=[SMEM] + [ANY] * (len(carried) + 2 * n_own),
        out_specs=ANY,
        scratch_shapes=[pltpu.SemaphoreType.DMA((2 * n_own,))],
        input_output_aliases={1: 0} if carried else {},
        cost_estimate=pl.CostEstimate(flops=0, bytes_accessed=4 * 2**20, transcendentals=0),
        name=f"lay_{wave}",
    )(place, *carried, *tiles)


def solution(mesh):
    n_strat = mesh.shape["strat"]
    n_grp = mesh.shape["grp"]
    at = list(range(0, n_grp, 2)) + list(range(n_grp - 1, 0, -2))
    ring = [
        [(at[r], at[(r + step) % n_grp]) for r in range(n_grp)] for step in (1, -1)
    ]
    last = [
        [
            (s * n_grp + i, ((s - 1) % n_strat) * n_grp + j)
            for s in range(n_strat)
            for i, j in hop
        ]
        for hop in ring
    ]
    turn = [(s, (s - 1) % n_strat) for s in range(n_strat)]

    def per_device(user_factors, item_factors, tile_coords, tile_counts, tile_values):
        coords = tile_coords[0, 0]
        counts = tile_counts[0, 0]
        values = tile_values[0, 0]
        rounds = coords.shape[0]
        side = values.shape[-1]
        width = user_factors.shape[1]
        g = lax.axis_index("grp").astype(jnp.int32)
        place = jnp.where(g % 2 == 0, g // 2, n_grp - 1 - g // 2).reshape(1)
        users = user_factors
        slab = item_factors.reshape(n_grp, 2 * WAVES, side, width)
        slabs = [[slab] for _ in range(WAVES)]
        for sub in range(rounds):
            final = sub + 1 == rounds
            after = users
            nexts = []
            for wave in range(WAVES):
                after, near_f, near_b, far, own = tile_step(
                    sub, wave, n_grp, coords, counts, place, users, after, slabs[wave], values
                )
                if not final:
                    own = lax.ppermute(own, "strat", turn)
                parts = [near_f, near_b]
                for t in range(1, n_grp):
                    for way in range(2):
                        part = parts[way]
                        if t > 1:
                            part = part + far[way, t - 2]
                        if t + 1 == n_grp and not final:
                            parts[way] = lax.ppermute(part, ("strat", "grp"), last[way])
                        else:
                            parts[way] = lax.ppermute(part, "grp", ring[way])
                got = [[own[way] + parts[way]] for way in range(2)]
                for t in range(1, n_grp):
                    for way in range(2):
                        got[way].append(lax.ppermute(got[way][-1], "grp", ring[way]))
                nexts.append(got[0] + got[1])
            users = after
            slabs = nexts
        items = None
        for wave in range(WAVES):
            items = lay(wave, n_grp, place, slabs[wave], items)
        return users, items.reshape(item_factors.shape)

    placed = (
        P(("strat", "grp"), None),
        P("strat", None),
        P("strat", "grp", None, None, None),
        P("strat", "grp", None),
        P("strat", "grp", None, None, None, None),
    )
    return jax.shard_map(
        per_device,
        mesh=mesh,
        in_specs=placed,
        out_specs=(P(("strat", "grp"), None), P("strat", None)),
        check_vma=False,
    )
```

```python
import functools

import jax
import jax.numpy as jnp
from jax import lax
from jax.experimental import pallas as pl
from jax.experimental.pallas import tpu as pltpu
from jax.sharding import PartitionSpec as P

RATE = 0.003
KEEP = 1.0 - 0.003 * 0.05
WAVES = 2
ANY = pl.BlockSpec(memory_space=pl.ANY)
VMEM = pl.BlockSpec(memory_space=pltpu.VMEM)
SMEM = pl.BlockSpec(memory_space=pltpu.SMEM)


def tile_kernel(sub, wave, side, n_own, *refs):
    fresh = sub == 0
    n_v = 1 if fresh else 2 * n_own
    coords, counts, place, users, running = refs[:5]
    slabs = refs[5 : 5 + n_v]
    values, out_u, near_f, near_b, far, own, held, grad, seen, sems = refs[5 + n_v :]

    copies = []

    def copy(src, dst):
        c = pltpu.make_async_copy(src, dst, sems.at[len(copies)])
        c.start()
        copies.append(c)

    copy(values.at[sub], seen)
    if fresh:
        for way in range(2):
            copy(
                slabs[0].at[:, 2 * wave + way],
                held.at[pl.ds(way * n_own, n_own)],
            )
    else:
        for i, tile in enumerate(slabs):
            held[i] = tile[...]
    grad[...] = jnp.zeros_like(grad)
    if wave == 0:
        out_u[...] = users[...] * KEEP
    else:
        out_u[...] = running[...]
    for c in copies:
        c.wait()

    here = place[0]
    count = counts[sub]

    def one(n, carry):
        a = coords[sub, 0, n]
        b = coords[sub, 1, n]

        @pl.when((n < count) & (((b >> 1) & 1) == wave))
        def _():
            owner = b >> 2
            way = b & 1
            ahead = jnp.where(way == 0, here - owner, owner - here)
            slot = way * n_own + lax.rem(ahead + n_own, n_own)
            source = way * n_own + owner if fresh else slot
            rows = pl.ds(pl.multiple_of(a * side, side), side)
            ua = users[rows, :].astype(jnp.bfloat16)
            vb = held[source].astype(jnp.bfloat16)
            guess = lax.dot_general(
                ua, vb, (((1,), (1,)), ((), ())), preferred_element_type=jnp.float32
            )
            resid = (seen[n].astype(jnp.float32) - guess).astype(jnp.bfloat16)
            up = jnp.dot(resid, vb, preferred_element_type=jnp.float32)
            out_u[rows, :] += RATE * up
            ip = lax.dot_general(
                resid, ua, (((0,), (0,)), ((), ())), preferred_element_type=jnp.float32
            )
            grad[slot] += RATE * ip

        return carry

    lax.fori_loop(0, coords.shape[2], one, 0)

    near_f[...] = grad[1]
    near_b[...] = grad[n_own + 1]
    for way in range(2):
        far[way] = grad[way * n_own + 2 : (way + 1) * n_own]
        source = way * n_own + here if fresh else way * n_own
        own[way] = held[source] * KEEP + grad[way * n_own]


def tile_step(sub, wave, n_own, coords, counts, place, users, running, slabs, values):
    side = values.shape[-1]
    width = users.shape[1]
    tile = jax.ShapeDtypeStruct((side, width), jnp.float32)
    slots = 2 * n_own
    return pl.pallas_call(
        functools.partial(tile_kernel, sub, wave, side, n_own),
        out_shape=(
            jax.ShapeDtypeStruct(users.shape, jnp.float32),
            tile,
            tile,
            jax.ShapeDtypeStruct((2, n_own - 2, side, width), jnp.float32),
            jax.ShapeDtypeStruct((2, side, width), jnp.float32),
        ),
        in_specs=[SMEM, SMEM, SMEM, VMEM, VMEM]
        + [VMEM if sub else ANY] * len(slabs)
        + [ANY],
        out_specs=(VMEM,) * 5,
        scratch_shapes=[
            pltpu.VMEM((slots, side, width), jnp.float32),
            pltpu.VMEM((slots, side, width), jnp.float32),
            pltpu.VMEM(values.shape[1:], values.dtype),
            pltpu.SemaphoreType.DMA((3,)),
        ],
        compiler_params=pltpu.CompilerParams(vmem_limit_bytes=24 * 2**20),
        cost_estimate=pl.CostEstimate(
            flops=8 * 3 * 2 * side * side * width,
            bytes_accessed=8 * 2**20,
            transcendentals=0,
        ),
        name=f"tiles_{sub}_{wave}",
    )(coords, counts, place, users, running, *slabs, values)


def lay_kernel(wave, n_own, carried, *refs):
    place = refs[0]
    tiles = refs[1 + carried : 1 + carried + 2 * n_own]
    out, sems = refs[1 + carried + 2 * n_own :]
    here = place[0]
    copies = []
    for way in range(2):
        for t in range(n_own):
            owner = lax.rem(here + (n_own - t if way == 0 else t), n_own)
            i = way * n_own + t
            c = pltpu.make_async_copy(tiles[i], out.at[owner, 2 * wave + way], sems.at[i])
            c.start()
            copies.append(c)
    for c in copies:
        c.wait()


def lay(wave, n_own, place, tiles, base):
    side, width = tiles[0].shape
    carried = () if base is None else (base,)
    return pl.pallas_call(
        functools.partial(lay_kernel, wave, n_own, len(carried)),
        out_shape=jax.ShapeDtypeStruct((n_own, 2 * WAVES, side, width), jnp.float32),
        in_specs=[SMEM] + [ANY] * len(carried) + [VMEM] * (2 * n_own),
        out_specs=ANY,
        scratch_shapes=[pltpu.SemaphoreType.DMA((2 * n_own,))],
        input_output_aliases={1: 0} if carried else {},
        cost_estimate=pl.CostEstimate(flops=0, bytes_accessed=4 * 2**20, transcendentals=0),
        name=f"lay_{wave}",
    )(place, *carried, *tiles)


def solution(mesh):
    n_strat = mesh.shape["strat"]
    n_grp = mesh.shape["grp"]
    at = list(range(0, n_grp, 2)) + list(range(n_grp - 1, 0, -2))
    ring = [
        [(at[r], at[(r + step) % n_grp]) for r in range(n_grp)] for step in (1, -1)
    ]
    last = [
        [
            (s * n_grp + i, ((s - 1) % n_strat) * n_grp + j)
            for s in range(n_strat)
            for i, j in hop
        ]
        for hop in ring
    ]
    turn = [(s, (s - 1) % n_strat) for s in range(n_strat)]

    def per_device(user_factors, item_factors, tile_coords, tile_counts, tile_values):
        coords = tile_coords[0, 0]
        counts = tile_counts[0, 0]
        values = tile_values[0, 0]
        rounds = coords.shape[0]
        side = values.shape[-1]
        width = user_factors.shape[1]
        g = lax.axis_index("grp").astype(jnp.int32)
        place = jnp.where(g % 2 == 0, g // 2, n_grp - 1 - g // 2).reshape(1)
        users = user_factors
        slab = item_factors.reshape(n_grp, 2 * WAVES, side, width)
        slabs = [[slab] for _ in range(WAVES)]
        for sub in range(rounds):
            final = sub + 1 == rounds
            after = users
            nexts = []
            for wave in range(WAVES):
                after, near_f, near_b, far, own = tile_step(
                    sub, wave, n_grp, coords, counts, place, users, after, slabs[wave], values
                )
                if not final:
                    own = lax.ppermute(own, "strat", turn)
                parts = [near_f, near_b]
                for t in range(1, n_grp):
                    for way in range(2):
                        part = parts[way]
                        if t > 1:
                            part = part + far[way, t - 2]
                        if t + 1 == n_grp and not final:
                            parts[way] = lax.ppermute(part, ("strat", "grp"), last[way])
                        else:
                            parts[way] = lax.ppermute(part, "grp", ring[way])
                got = [[own[way] + parts[way]] for way in range(2)]
                for t in range(1, n_grp):
                    for way in range(2):
                        got[way].append(lax.ppermute(got[way][-1], "grp", ring[way]))
                nexts.append(got[0] + got[1])
            users = after
            slabs = nexts
        items = None
        for wave in range(WAVES):
            items = lay(wave, n_grp, place, slabs[wave], items)
        return users, items.reshape(item_factors.shape)

    placed = (
        P(("strat", "grp"), None),
        P("strat", None),
        P("strat", "grp", None, None, None),
        P("strat", "grp", None),
        P("strat", "grp", None, None, None, None),
    )
    return jax.shard_map(
        per_device,
        mesh=mesh,
        in_specs=placed,
        out_specs=(P(("strat", "grp"), None), P("strat", None)),
        check_vma=False,
    )
```

```python
import functools

import jax
import jax.numpy as jnp
from jax import lax
from jax.experimental import pallas as pl
from jax.experimental.pallas import tpu as pltpu
from jax.sharding import PartitionSpec as P

RATE = 0.003
KEEP = 1.0 - 0.003 * 0.05
WAVES = 2
GROUP = 4
ANY = pl.BlockSpec(memory_space=pl.ANY)
HBM = pl.BlockSpec(memory_space=pltpu.HBM)
VMEM = pl.BlockSpec(memory_space=pltpu.VMEM)
SMEM = pl.BlockSpec(memory_space=pltpu.SMEM)


def tile_kernel(sub, wave, side, n_own, *refs):
    fresh = sub == 0
    refs = list(refs)
    coords, counts, place, users = (refs.pop(0) for _ in range(4))
    running = refs.pop(0) if wave else None
    slabs = [refs.pop(0) for _ in range(1 if fresh else 2 * n_own)]
    values, out_u, near_f, near_b, far_f, far_b, own = (refs.pop(0) for _ in range(7))
    held, grad, seen, order, sems = (refs.pop(0) for _ in range(5))

    copies = []

    def copy(src, dst):
        c = pltpu.make_async_copy(src, dst, sems.at[len(copies)])
        c.start()
        copies.append(c)

    if fresh:
        (mine,) = refs
        copy(users, mine)
        users = mine
        for way in range(2):
            copy(
                slabs[0].at[:, 2 * wave + way],
                held.at[pl.ds(way * n_own, n_own)],
            )
    copy(values.at[sub], seen)
    if not fresh:
        for i, tile in enumerate(slabs):
            held[i] = tile[...]
    grad[...] = jnp.zeros_like(grad)

    count = counts[sub]

    def gather(n, total):
        order[total] = n
        hit = (n < count) & (((coords[sub, 1, n] >> 1) & 1) == wave)
        return total + hit.astype(jnp.int32)

    total = lax.fori_loop(0, coords.shape[2], gather, 0)
    for c in copies:
        c.wait()
    out_u[...] = running[...] if wave else users[...] * KEEP
    here = place[0]

    def some(i, carry):
        done = []
        for j in range(GROUP):
            at = i * GROUP + j
            n = order[jnp.minimum(at, total - 1)]
            rate = jnp.where(at < total, RATE, 0.0)
            a = coords[sub, 0, n]
            b = coords[sub, 1, n]
            owner = b >> 2
            way = b & 1
            ahead = jnp.where(way == 0, here - owner, owner - here)
            slot = way * n_own + lax.rem(ahead + n_own, n_own)
            source = way * n_own + owner if fresh else slot
            rows = pl.ds(pl.multiple_of(a * side, side), side)
            ua = users[rows, :].astype(jnp.bfloat16)
            vb = held[source].astype(jnp.bfloat16)
            guess = lax.dot_general(
                ua, vb, (((1,), (1,)), ((), ())), preferred_element_type=jnp.float32
            )
            resid = (seen[n].astype(jnp.float32) - guess).astype(jnp.bfloat16)
            up = jnp.dot(resid, vb, preferred_element_type=jnp.float32)
            ip = lax.dot_general(
                resid, ua, (((0,), (0,)), ((), ())), preferred_element_type=jnp.float32
            )
            done.append((rows, slot, rate * up, rate * ip))
        for rows, slot, up, ip in done:
            out_u[rows, :] += up
            grad[slot] += ip
        return carry

    lax.fori_loop(0, (total + GROUP - 1) // GROUP, some, 0)

    near_f[...] = grad[1]
    near_b[...] = grad[n_own + 1]
    far_f[...] = grad[2:n_own]
    far_b[...] = grad[n_own + 2 : 2 * n_own]
    for way in range(2):
        source = way * n_own + here if fresh else way * n_own
        own[way] = held[source] * KEEP + grad[way * n_own]


def tile_step(sub, wave, n_own, coords, counts, place, users, running, slabs, values):
    side = values.shape[-1]
    width = users.shape[1]
    tile = jax.ShapeDtypeStruct((side, width), jnp.float32)
    far = jax.ShapeDtypeStruct((n_own - 2, side, width), jnp.float32)
    slots = 2 * n_own
    carried = (running,) if wave else ()
    return pl.pallas_call(
        functools.partial(tile_kernel, sub, wave, side, n_own),
        out_shape=(
            jax.ShapeDtypeStruct(users.shape, jnp.float32),
            tile,
            tile,
            far,
            far,
            jax.ShapeDtypeStruct((2, side, width), jnp.float32),
        ),
        in_specs=[SMEM, SMEM, SMEM, VMEM if sub else HBM]
        + [VMEM] * len(carried)
        + [VMEM if sub else HBM] * len(slabs)
        + [HBM],
        out_specs=(VMEM,) * 6,
        input_output_aliases={4: 0} if wave else {},
        scratch_shapes=[
            pltpu.VMEM((slots, side, width), jnp.float32),
            pltpu.VMEM((slots, side, width), jnp.float32),
            pltpu.VMEM(values.shape[1:], values.dtype),
            pltpu.SMEM((coords.shape[2] + 1,), jnp.int32),
            pltpu.SemaphoreType.DMA((4,)),
        ]
        + ([] if sub else [pltpu.VMEM(users.shape, jnp.float32)]),
        compiler_params=pltpu.CompilerParams(vmem_limit_bytes=(50 if sub + wave == 0 else 24) * 2**20),
        cost_estimate=pl.CostEstimate(
            flops=8 * 3 * 2 * side * side * width,
            bytes_accessed=8 * 2**20,
            transcendentals=0,
        ),
        name=f"tiles_{sub}_{wave}",
    )(coords, counts, place, users, *carried, *slabs, values)


def lay_kernel(wave, n_own, carried, *refs):
    place = refs[0]
    tiles = refs[1 + carried : 1 + carried + 2 * n_own]
    out, sems = refs[1 + carried + 2 * n_own :]
    here = place[0]
    copies = []
    for way in range(2):
        for t in range(n_own):
            owner = lax.rem(here + (n_own - t if way == 0 else t), n_own)
            i = way * n_own + t
            c = pltpu.make_async_copy(tiles[i], out.at[owner, 2 * wave + way], sems.at[i])
            c.start()
            copies.append(c)
    for c in copies:
        c.wait()


def lay(wave, n_own, place, tiles, base):
    side, width = tiles[0].shape
    carried = () if base is None else (base,)
    return pl.pallas_call(
        functools.partial(lay_kernel, wave, n_own, len(carried)),
        out_shape=jax.ShapeDtypeStruct((n_own, 2 * WAVES, side, width), jnp.float32),
        in_specs=[SMEM] + [ANY] * len(carried) + [VMEM] * (2 * n_own),
        out_specs=ANY,
        scratch_shapes=[pltpu.SemaphoreType.DMA((2 * n_own,))],
        input_output_aliases={1: 0} if carried else {},
        compiler_params=pltpu.CompilerParams(vmem_limit_bytes=16 * 2**20),
        cost_estimate=pl.CostEstimate(flops=0, bytes_accessed=4 * 2**20, transcendentals=0),
        name=f"lay_{wave}",
    )(place, *carried, *tiles)


def solution(mesh):
    n_strat = mesh.shape["strat"]
    n_grp = mesh.shape["grp"]
    at = list(range(0, n_grp, 2)) + list(range(n_grp - 1, 0, -2))
    ring = [
        [(at[r], at[(r + step) % n_grp]) for r in range(n_grp)] for step in (1, -1)
    ]
    last = [
        [
            (s * n_grp + i, ((s - 1) % n_strat) * n_grp + j)
            for s in range(n_strat)
            for i, j in hop
        ]
        for hop in ring
    ]
    turn = [(s, (s - 1) % n_strat) for s in range(n_strat)]

    def per_device(user_factors, item_factors, tile_coords, tile_counts, tile_values):
        coords = tile_coords[0, 0]
        counts = tile_counts[0, 0]
        values = tile_values[0, 0]
        rounds = coords.shape[0]
        side = values.shape[-1]
        width = user_factors.shape[1]
        g = lax.axis_index("grp").astype(jnp.int32)
        place = jnp.where(g % 2 == 0, g // 2, n_grp - 1 - g // 2).reshape(1)
        users = user_factors
        slab = item_factors.reshape(n_grp, 2 * WAVES, side, width)
        slabs = [[slab] for _ in range(WAVES)]
        for sub in range(rounds):
            final = sub + 1 == rounds
            after = None
            sums = []
            owns = []
            for wave in range(WAVES):
                after, *near, far_f, far_b, own = tile_step(
                    sub, wave, n_grp, coords, counts, place, users, after, slabs[wave], values
                )
                sums.append((near, (far_f, far_b)))
                owns.append(own)
            if not final:
                owns = [lax.ppermute(own, "strat", turn) for own in owns]
            owns = [[lax.optimization_barrier(own[way]) for way in range(2)] for own in owns]
            nexts = []
            for wave in range(WAVES):
                parts, far = sums[wave]
                for t in range(1, n_grp):
                    for way in range(2):
                        part = parts[way]
                        if t > 1:
                            part = part + far[way][t - 2]
                        if t + 1 == n_grp and not final:
                            parts[way] = lax.ppermute(part, ("strat", "grp"), last[way])
                        else:
                            parts[way] = lax.ppermute(part, "grp", ring[way])
                got = [[owns[wave][way] + parts[way]] for way in range(2)]
                for t in range(1, n_grp):
                    for way in range(2):
                        got[way].append(lax.ppermute(got[way][-1], "grp", ring[way]))
                nexts.append(got[0] + got[1])
            users = after
            slabs = nexts
        items = None
        for wave in range(WAVES):
            items = lay(wave, n_grp, place, slabs[wave], items)
        return users, items.reshape(item_factors.shape)

    placed = (
        P(("strat", "grp"), None),
        P("strat", None),
        P("strat", "grp", None, None, None),
        P("strat", "grp", None),
        P("strat", "grp", None, None, None, None),
    )
    return jax.shard_map(
        per_device,
        mesh=mesh,
        in_specs=placed,
        out_specs=(P(("strat", "grp"), None), P("strat", None)),
        check_vma=False,
    )
```

```python
import functools

import jax
import jax.numpy as jnp
from jax import lax
from jax.experimental import pallas as pl
from jax.experimental.pallas import tpu as pltpu
from jax.sharding import PartitionSpec as P

RATE = 0.003
KEEP = 1.0 - 0.003 * 0.05
WAVES = 2
FLOWS = 2 * WAVES
GROUP = 4
ANY = pl.BlockSpec(memory_space=pl.ANY)
HBM = pl.BlockSpec(memory_space=pltpu.HBM)
VMEM = pl.BlockSpec(memory_space=pltpu.VMEM)
SMEM = pl.BlockSpec(memory_space=pltpu.SMEM)


def tile_kernel(sub, side, n_own, *refs):
    refs = list(refs)
    coords, counts, place, users = (refs.pop(0) for _ in range(4))
    slabs = [refs.pop(0) for _ in range(FLOWS * n_own)]
    values, out_u = (refs.pop(0) for _ in range(2))
    near = [refs.pop(0) for _ in range(FLOWS)]
    far = [refs.pop(0) for _ in range(FLOWS)]
    owns = [refs.pop(0) for _ in range(WAVES)]
    held, grad, seen, sem = refs
    here = place[0]
    count = counts[sub]

    copy = pltpu.make_async_copy(values.at[sub], seen, sem)
    copy.start()
    for i, tile in enumerate(slabs):
        held[i] = tile[...]
    grad[...] = jnp.zeros_like(grad)
    copy.wait()
    out_u[...] = users[...] * KEEP

    def some(i, carry):
        done = []
        for j in range(GROUP):
            at = i * GROUP + j
            n = jnp.minimum(at, count - 1)
            rate = jnp.where(at < count, RATE, 0.0)
            a = coords[sub, 0, n]
            b = coords[sub, 1, n]
            owner = b >> 2
            flow = b & 3
            ahead = jnp.where((b & 1) == 0, here - owner, owner - here)
            slot = flow * n_own + lax.rem(ahead + n_own, n_own)
            rows = pl.ds(pl.multiple_of(a * side, side), side)
            ua = users[rows, :].astype(jnp.bfloat16)
            vb = held[slot].astype(jnp.bfloat16)
            guess = lax.dot_general(
                ua, vb, (((1,), (1,)), ((), ())), preferred_element_type=jnp.float32
            )
            resid = (seen[n].astype(jnp.float32) - guess).astype(jnp.bfloat16)
            up = jnp.dot(resid, vb, preferred_element_type=jnp.float32)
            ip = lax.dot_general(
                resid, ua, (((0,), (0,)), ((), ())), preferred_element_type=jnp.float32
            )
            done.append((rows, slot, rate * up, rate * ip))
        for rows, slot, up, ip in done:
            out_u[rows, :] += up
            grad[slot] += ip
        return carry

    lax.fori_loop(0, (count + GROUP - 1) // GROUP, some, 0)

    for flow in range(FLOWS):
        mine = flow * n_own
        near[flow][...] = grad[mine + 1]
        far[flow][...] = grad[mine + 2 : mine + n_own]
        owns[flow // 2][flow & 1] = held[mine] * KEEP + grad[mine]


def tile_step(sub, n_own, coords, counts, place, users, slabs, values):
    side = values.shape[-1]
    width = users.shape[1]

    def tiles(*lead):
        return jax.ShapeDtypeStruct((*lead, side, width), jnp.float32)

    tails = (tiles(),) * FLOWS + (tiles(n_own - 2),) * FLOWS + (tiles(2),) * WAVES
    return pl.pallas_call(
        functools.partial(tile_kernel, sub, side, n_own),
        out_shape=(jax.ShapeDtypeStruct(users.shape, jnp.float32), *tails),
        in_specs=[SMEM, SMEM, SMEM, VMEM] + [VMEM] * len(slabs) + [HBM],
        out_specs=(VMEM,) * (1 + len(tails)),
        scratch_shapes=[
            pltpu.VMEM((FLOWS * n_own, side, width), jnp.float32),
            pltpu.VMEM((FLOWS * n_own, side, width), jnp.float32),
            pltpu.VMEM(values.shape[1:], values.dtype),
            pltpu.SemaphoreType.DMA,
        ],
        compiler_params=pltpu.CompilerParams(vmem_limit_bytes=24 * 2**20),
        cost_estimate=pl.CostEstimate(
            flops=16 * 3 * 2 * side * side * width,
            bytes_accessed=16 * 2**20,
            transcendentals=0,
        ),
        name=f"tiles_{sub}",
    )(coords, counts, place, users, *slabs, values)


def first_kernel(wave, side, n_own, *refs):
    refs = list(refs)
    coords, counts, place, users = (refs.pop(0) for _ in range(4))
    running = refs.pop(0) if wave else None
    slab = refs.pop(0)
    values, out_u, near_f, near_b, far_f, far_b, own = (refs.pop(0) for _ in range(7))
    held, grad, seen, order, sems, mine = refs

    copies = []

    def copy(src, dst):
        c = pltpu.make_async_copy(src, dst, sems.at[len(copies)])
        c.start()
        copies.append(c)

    copy(users, mine)
    users = mine
    for way in range(2):
        copy(slab.at[:, 2 * wave + way], held.at[pl.ds(way * n_own, n_own)])
    copy(values.at[0], seen)
    grad[...] = jnp.zeros_like(grad)

    count = counts[0]

    def gather(n, total):
        order[total] = n
        hit = (n < count) & (((coords[0, 1, n] >> 1) & 1) == wave)
        return total + hit.astype(jnp.int32)

    total = lax.fori_loop(0, coords.shape[2], gather, 0)
    for c in copies:
        c.wait()
    out_u[...] = running[...] if wave else users[...] * KEEP
    here = place[0]

    def some(i, carry):
        done = []
        for j in range(GROUP):
            at = i * GROUP + j
            n = order[jnp.minimum(at, total - 1)]
            rate = jnp.where(at < total, RATE, 0.0)
            a = coords[0, 0, n]
            b = coords[0, 1, n]
            owner = b >> 2
            way = b & 1
            ahead = jnp.where(way == 0, here - owner, owner - here)
            slot = way * n_own + lax.rem(ahead + n_own, n_own)
            source = way * n_own + owner
            rows = pl.ds(pl.multiple_of(a * side, side), side)
            ua = users[rows, :].astype(jnp.bfloat16)
            vb = held[source].astype(jnp.bfloat16)
            guess = lax.dot_general(
                ua, vb, (((1,), (1,)), ((), ())), preferred_element_type=jnp.float32
            )
            resid = (seen[n].astype(jnp.float32) - guess).astype(jnp.bfloat16)
            up = jnp.dot(resid, vb, preferred_element_type=jnp.float32)
            ip = lax.dot_general(
                resid, ua, (((0,), (0,)), ((), ())), preferred_element_type=jnp.float32
            )
            done.append((rows, slot, rate * up, rate * ip))
        for rows, slot, up, ip in done:
            out_u[rows, :] += up
            grad[slot] += ip
        return carry

    lax.fori_loop(0, (total + GROUP - 1) // GROUP, some, 0)

    near_f[...] = grad[1]
    near_b[...] = grad[n_own + 1]
    far_f[...] = grad[2:n_own]
    far_b[...] = grad[n_own + 2 : 2 * n_own]
    for way in range(2):
        own[way] = held[way * n_own + here] * KEEP + grad[way * n_own]


def first_step(wave, n_own, coords, counts, place, users, running, slab, values):
    side = values.shape[-1]
    width = users.shape[1]
    tile = jax.ShapeDtypeStruct((side, width), jnp.float32)
    far = jax.ShapeDtypeStruct((n_own - 2, side, width), jnp.float32)
    slots = 2 * n_own
    carried = (running,) if wave else ()
    return pl.pallas_call(
        functools.partial(first_kernel, wave, side, n_own),
        out_shape=(
            jax.ShapeDtypeStruct(users.shape, jnp.float32),
            tile,
            tile,
            far,
            far,
            jax.ShapeDtypeStruct((2, side, width), jnp.float32),
        ),
        in_specs=[SMEM, SMEM, SMEM, HBM] + [VMEM] * len(carried) + [HBM, HBM],
        out_specs=(VMEM,) * 6,
        input_output_aliases={4: 0} if wave else {},
        scratch_shapes=[
            pltpu.VMEM((slots, side, width), jnp.float32),
            pltpu.VMEM((slots, side, width), jnp.float32),
            pltpu.VMEM(values.shape[1:], values.dtype),
            pltpu.SMEM((coords.shape[2] + 1,), jnp.int32),
            pltpu.SemaphoreType.DMA((4,)),
            pltpu.VMEM(users.shape, jnp.float32),
        ],
        compiler_params=pltpu.CompilerParams(vmem_limit_bytes=(24 if wave else 50) * 2**20),
        cost_estimate=pl.CostEstimate(
            flops=8 * 3 * 2 * side * side * width,
            bytes_accessed=8 * 2**20,
            transcendentals=0,
        ),
        name=f"tiles_0_{wave}",
    )(coords, counts, place, users, *carried, slab, values)


def lay_kernel(wave, n_own, carried, *refs):
    place = refs[0]
    tiles = refs[1 + carried : 1 + carried + 2 * n_own]
    out, sems = refs[1 + carried + 2 * n_own :]
    here = place[0]
    copies = []
    for way in range(2):
        for t in range(n_own):
            owner = lax.rem(here + (n_own - t if way == 0 else t), n_own)
            i = way * n_own + t
            c = pltpu.make_async_copy(tiles[i], out.at[owner, 2 * wave + way], sems.at[i])
            c.start()
            copies.append(c)
    for c in copies:
        c.wait()


def lay(wave, n_own, place, tiles, base):
    side, width = tiles[0].shape
    carried = () if base is None else (base,)
    return pl.pallas_call(
        functools.partial(lay_kernel, wave, n_own, len(carried)),
        out_shape=jax.ShapeDtypeStruct((n_own, 2 * WAVES, side, width), jnp.float32),
        in_specs=[SMEM] + [ANY] * len(carried) + [VMEM] * (2 * n_own),
        out_specs=ANY,
        scratch_shapes=[pltpu.SemaphoreType.DMA((2 * n_own,))],
        input_output_aliases={1: 0} if carried else {},
        compiler_params=pltpu.CompilerParams(vmem_limit_bytes=16 * 2**20),
        cost_estimate=pl.CostEstimate(flops=0, bytes_accessed=4 * 2**20, transcendentals=0),
        name=f"lay_{wave}",
    )(place, *carried, *tiles)


def solution(mesh):
    n_strat = mesh.shape["strat"]
    n_grp = mesh.shape["grp"]
    at = list(range(0, n_grp, 2)) + list(range(n_grp - 1, 0, -2))
    ring = [
        [(at[r], at[(r + step) % n_grp]) for r in range(n_grp)] for step in (1, -1)
    ]
    last = [
        [
            (s * n_grp + i, ((s - 1) % n_strat) * n_grp + j)
            for s in range(n_strat)
            for i, j in hop
        ]
        for hop in ring
    ]
    turn = [(s, (s - 1) % n_strat) for s in range(n_strat)]

    def per_device(user_factors, item_factors, tile_coords, tile_counts, tile_values):
        coords = tile_coords[0, 0]
        counts = tile_counts[0, 0]
        values = tile_values[0, 0]
        rounds = coords.shape[0]
        side = values.shape[-1]
        width = user_factors.shape[1]
        g = lax.axis_index("grp").astype(jnp.int32)
        place = jnp.where(g % 2 == 0, g // 2, n_grp - 1 - g // 2).reshape(1)
        users = user_factors
        slab = item_factors.reshape(n_grp, FLOWS, side, width)
        slabs = None
        for sub in range(rounds):
            final = sub + 1 == rounds
            if sub == 0:
                after = None
                sums = []
                owns = []
                for wave in range(WAVES):
                    after, *near, far_f, far_b, own = first_step(
                        wave, n_grp, coords, counts, place, users, after, slab, values
                    )
                    sums.append((near, (far_f, far_b)))
                    owns.append(own)
            else:
                after, *tails = tile_step(
                    sub, n_grp, coords, counts, place, users, slabs, values
                )
                owns = tails[2 * FLOWS :]
                sums = [
                    (tails[2 * w : 2 * w + 2], tails[FLOWS + 2 * w : FLOWS + 2 * w + 2])
                    for w in range(WAVES)
                ]
            if not final:
                owns = [lax.ppermute(own, "strat", turn) for own in owns]
            owns = [[lax.optimization_barrier(own[way]) for way in range(2)] for own in owns]
            nexts = []
            for wave in range(WAVES):
                parts, far = sums[wave]
                for t in range(1, n_grp):
                    for way in range(2):
                        part = parts[way]
                        if t > 1:
                            part = part + far[way][t - 2]
                        if t + 1 == n_grp and not final:
                            parts[way] = lax.ppermute(part, ("strat", "grp"), last[way])
                        else:
                            parts[way] = lax.ppermute(part, "grp", ring[way])
                got = [[owns[wave][way] + parts[way]] for way in range(2)]
                for t in range(1, n_grp):
                    for way in range(2):
                        got[way].append(lax.ppermute(got[way][-1], "grp", ring[way]))
                nexts += got[0] + got[1]
            users = after
            slabs = nexts
        items = None
        for wave in range(WAVES):
            tiles = slabs[2 * n_grp * wave : 2 * n_grp * (wave + 1)]
            items = lay(wave, n_grp, place, tiles, items)
        return users, items.reshape(item_factors.shape)

    placed = (
        P(("strat", "grp"), None),
        P("strat", None),
        P("strat", "grp", None, None, None),
        P("strat", "grp", None),
        P("strat", "grp", None, None, None, None),
    )
    return jax.shard_map(
        per_device,
        mesh=mesh,
        in_specs=placed,
        out_specs=(P(("strat", "grp"), None), P("strat", None)),
        check_vma=False,
    )
```

```python
import functools

import jax
import jax.numpy as jnp
from jax import lax
from jax.experimental import pallas as pl
from jax.experimental.pallas import tpu as pltpu
from jax.sharding import PartitionSpec as P

RATE = 0.003
KEEP = 1.0 - 0.003 * 0.05
WAVES = 2
FLOWS = 2 * WAVES
GROUP = 4
ANY = pl.BlockSpec(memory_space=pl.ANY)
HBM = pl.BlockSpec(memory_space=pltpu.HBM)
VMEM = pl.BlockSpec(memory_space=pltpu.VMEM)
SMEM = pl.BlockSpec(memory_space=pltpu.SMEM)


def tile_kernel(sub, side, n_own, *refs):
    refs = list(refs)
    coords, counts, place, users = (refs.pop(0) for _ in range(4))
    slabs = [refs.pop(0) for _ in range(FLOWS * n_own)]
    values, out_u = (refs.pop(0) for _ in range(2))
    near = [refs.pop(0) for _ in range(FLOWS)]
    far = [refs.pop(0) for _ in range(FLOWS)]
    owns = [refs.pop(0) for _ in range(WAVES)]
    held, grad, seen, sem = refs
    here = place[0]
    count = counts[sub]

    copy = pltpu.make_async_copy(values.at[sub], seen, sem)
    copy.start()
    for i, tile in enumerate(slabs):
        held[i] = tile[...]
    grad[...] = jnp.zeros_like(grad)
    copy.wait()
    out_u[...] = users[...] * KEEP

    def some(i, carry):
        done = []
        for j in range(GROUP):
            at = i * GROUP + j
            n = jnp.minimum(at, count - 1)
            rate = jnp.where(at < count, RATE, 0.0)
            a = coords[sub, 0, n]
            b = coords[sub, 1, n]
            owner = b >> 2
            flow = b & 3
            ahead = jnp.where((b & 1) == 0, here - owner, owner - here)
            slot = flow * n_own + lax.rem(ahead + n_own, n_own)
            rows = pl.ds(pl.multiple_of(a * side, side), side)
            ua = users[rows, :].astype(jnp.bfloat16)
            vb = held[slot].astype(jnp.bfloat16)
            guess = lax.dot_general(
                ua, vb, (((1,), (1,)), ((), ())), preferred_element_type=jnp.float32
            )
            resid = (seen[n].astype(jnp.float32) - guess).astype(jnp.bfloat16)
            up = jnp.dot(resid, vb, preferred_element_type=jnp.float32)
            ip = lax.dot_general(
                resid, ua, (((0,), (0,)), ((), ())), preferred_element_type=jnp.float32
            )
            done.append((rows, slot, rate * up, rate * ip))
        for rows, slot, up, ip in done:
            out_u[rows, :] += up
            grad[slot] += ip
        return carry

    lax.fori_loop(0, (count + GROUP - 1) // GROUP, some, 0)

    for flow in range(FLOWS):
        mine = flow * n_own
        near[flow][...] = grad[mine + 1]
        far[flow][...] = grad[mine + 2 : mine + n_own]
        owns[flow // 2][flow & 1] = held[mine] * KEEP + grad[mine]


def tile_step(sub, n_own, coords, counts, place, users, slabs, values):
    side = values.shape[-1]
    width = users.shape[1]

    def tiles(*lead):
        return jax.ShapeDtypeStruct((*lead, side, width), jnp.float32)

    tails = (tiles(),) * FLOWS + (tiles(n_own - 2),) * FLOWS + (tiles(2),) * WAVES
    return pl.pallas_call(
        functools.partial(tile_kernel, sub, side, n_own),
        out_shape=(jax.ShapeDtypeStruct(users.shape, jnp.float32), *tails),
        in_specs=[SMEM, SMEM, SMEM, VMEM] + [VMEM] * len(slabs) + [HBM],
        out_specs=(VMEM,) * (1 + len(tails)),
        scratch_shapes=[
            pltpu.VMEM((FLOWS * n_own, side, width), jnp.float32),
            pltpu.VMEM((FLOWS * n_own, side, width), jnp.float32),
            pltpu.VMEM(values.shape[1:], values.dtype),
            pltpu.SemaphoreType.DMA,
        ],
        compiler_params=pltpu.CompilerParams(vmem_limit_bytes=24 * 2**20),
        cost_estimate=pl.CostEstimate(
            flops=16 * 3 * 2 * side * side * width,
            bytes_accessed=16 * 2**20,
            transcendentals=0,
        ),
        name=f"tiles_{sub}",
    )(coords, counts, place, users, *slabs, values)


def first_kernel(wave, side, n_own, *refs):
    refs = list(refs)
    coords, counts, place, users = (refs.pop(0) for _ in range(4))
    running = refs.pop(0) if wave else None
    slab = refs.pop(0)
    values, out_u, near_f, near_b, far_f, far_b, own = (refs.pop(0) for _ in range(7))
    held, grad, seen, order, sems, mine = refs

    copies = []

    def copy(src, dst):
        c = pltpu.make_async_copy(src, dst, sems.at[len(copies)])
        c.start()
        copies.append(c)

    copy(users, mine)
    users = mine
    for way in range(2):
        copy(slab.at[:, 2 * wave + way], held.at[pl.ds(way * n_own, n_own)])
    copy(values.at[0], seen)
    grad[...] = jnp.zeros_like(grad)

    count = counts[0]

    def gather(n, total):
        order[total] = n
        hit = (n < count) & (((coords[0, 1, n] >> 1) & 1) == wave)
        return total + hit.astype(jnp.int32)

    total = lax.fori_loop(0, coords.shape[2], gather, 0)
    for c in copies:
        c.wait()
    out_u[...] = running[...] if wave else users[...] * KEEP
    here = place[0]

    def some(i, carry):
        done = []
        for j in range(GROUP):
            at = i * GROUP + j
            n = order[jnp.minimum(at, total - 1)]
            rate = jnp.where(at < total, RATE, 0.0)
            a = coords[0, 0, n]
            b = coords[0, 1, n]
            owner = b >> 2
            way = b & 1
            ahead = jnp.where(way == 0, here - owner, owner - here)
            slot = way * n_own + lax.rem(ahead + n_own, n_own)
            source = way * n_own + owner
            rows = pl.ds(pl.multiple_of(a * side, side), side)
            ua = users[rows, :].astype(jnp.bfloat16)
            vb = held[source].astype(jnp.bfloat16)
            guess = lax.dot_general(
                ua, vb, (((1,), (1,)), ((), ())), preferred_element_type=jnp.float32
            )
            resid = (seen[n].astype(jnp.float32) - guess).astype(jnp.bfloat16)
            up = jnp.dot(resid, vb, preferred_element_type=jnp.float32)
            ip = lax.dot_general(
                resid, ua, (((0,), (0,)), ((), ())), preferred_element_type=jnp.float32
            )
            done.append((rows, slot, rate * up, rate * ip))
        for rows, slot, up, ip in done:
            out_u[rows, :] += up
            grad[slot] += ip
        return carry

    lax.fori_loop(0, (total + GROUP - 1) // GROUP, some, 0)

    near_f[...] = grad[1]
    near_b[...] = grad[n_own + 1]
    far_f[...] = grad[2:n_own]
    far_b[...] = grad[n_own + 2 : 2 * n_own]
    for way in range(2):
        own[way] = held[way * n_own + here] * KEEP + grad[way * n_own]


def first_step(wave, n_own, coords, counts, place, users, running, slab, values):
    side = values.shape[-1]
    width = users.shape[1]
    tile = jax.ShapeDtypeStruct((side, width), jnp.float32)
    far = jax.ShapeDtypeStruct((n_own - 2, side, width), jnp.float32)
    slots = 2 * n_own
    carried = (running,) if wave else ()
    return pl.pallas_call(
        functools.partial(first_kernel, wave, side, n_own),
        out_shape=(
            jax.ShapeDtypeStruct(users.shape, jnp.float32),
            tile,
            tile,
            far,
            far,
            jax.ShapeDtypeStruct((2, side, width), jnp.float32),
        ),
        in_specs=[SMEM, SMEM, SMEM, HBM] + [VMEM] * len(carried) + [HBM, HBM],
        out_specs=(VMEM,) * 6,
        input_output_aliases={4: 0} if wave else {},
        scratch_shapes=[
            pltpu.VMEM((slots, side, width), jnp.float32),
            pltpu.VMEM((slots, side, width), jnp.float32),
            pltpu.VMEM(values.shape[1:], values.dtype),
            pltpu.SMEM((coords.shape[2] + 1,), jnp.int32),
            pltpu.SemaphoreType.DMA((4,)),
            pltpu.VMEM(users.shape, jnp.float32),
        ],
        compiler_params=pltpu.CompilerParams(vmem_limit_bytes=(24 if wave else 50) * 2**20),
        cost_estimate=pl.CostEstimate(
            flops=8 * 3 * 2 * side * side * width,
            bytes_accessed=8 * 2**20,
            transcendentals=0,
        ),
        name=f"tiles_0_{wave}",
    )(coords, counts, place, users, *carried, slab, values)


def lay_kernel(wave, n_own, carried, *refs):
    place = refs[0]
    tiles = refs[1 + carried : 1 + carried + 2 * n_own]
    out, sems = refs[1 + carried + 2 * n_own :]
    here = place[0]
    copies = []
    for way in range(2):
        for t in range(n_own):
            owner = lax.rem(here + (n_own - t if way == 0 else t), n_own)
            i = way * n_own + t
            c = pltpu.make_async_copy(tiles[i], out.at[owner, 2 * wave + way], sems.at[i])
            c.start()
            copies.append(c)
    for c in copies:
        c.wait()


def lay(wave, n_own, place, tiles, base):
    side, width = tiles[0].shape
    carried = () if base is None else (base,)
    return pl.pallas_call(
        functools.partial(lay_kernel, wave, n_own, len(carried)),
        out_shape=jax.ShapeDtypeStruct((n_own, 2 * WAVES, side, width), jnp.float32),
        in_specs=[SMEM] + [ANY] * len(carried) + [VMEM] * (2 * n_own),
        out_specs=ANY,
        scratch_shapes=[pltpu.SemaphoreType.DMA((2 * n_own,))],
        input_output_aliases={1: 0} if carried else {},
        compiler_params=pltpu.CompilerParams(vmem_limit_bytes=16 * 2**20),
        cost_estimate=pl.CostEstimate(flops=0, bytes_accessed=4 * 2**20, transcendentals=0),
        name=f"lay_{wave}",
    )(place, *carried, *tiles)


def solution(mesh):
    n_strat = mesh.shape["strat"]
    n_grp = mesh.shape["grp"]
    at = list(range(0, n_grp, 2)) + list(range(n_grp - 1, 0, -2))
    ring = [
        [(at[r], at[(r + step) % n_grp]) for r in range(n_grp)] for step in (1, -1)
    ]
    last = [
        [
            (s * n_grp + i, ((s - 1) % n_strat) * n_grp + j)
            for s in range(n_strat)
            for i, j in hop
        ]
        for hop in ring
    ]
    turn = [(s, (s - 1) % n_strat) for s in range(n_strat)]

    def per_device(user_factors, item_factors, tile_coords, tile_counts, tile_values):
        coords = tile_coords[0, 0]
        counts = tile_counts[0, 0]
        values = tile_values[0, 0]
        rounds = coords.shape[0]
        side = values.shape[-1]
        width = user_factors.shape[1]
        g = lax.axis_index("grp").astype(jnp.int32)
        place = jnp.where(g % 2 == 0, g // 2, n_grp - 1 - g // 2).reshape(1)
        users = user_factors
        slab = item_factors.reshape(n_grp, FLOWS, side, width)
        slabs = None
        for sub in range(rounds):
            final = sub + 1 == rounds
            if sub == 0:
                after = None
                sums = []
                owns = []
                for wave in range(WAVES):
                    after, *near, far_f, far_b, own = first_step(
                        wave, n_grp, coords, counts, place, users, after, slab, values
                    )
                    sums.append((near, (far_f, far_b)))
                    owns.append(own)
            else:
                after, *tails = tile_step(
                    sub, n_grp, coords, counts, place, users, slabs, values
                )
                owns = tails[2 * FLOWS :]
                sums = [
                    (tails[2 * w : 2 * w + 2], tails[FLOWS + 2 * w : FLOWS + 2 * w + 2])
                    for w in range(WAVES)
                ]
            if not final:
                owns = [lax.ppermute(own, "strat", turn) for own in owns]
            owns = [[lax.optimization_barrier(own[way]) for way in range(2)] for own in owns]
            for t in range(1, n_grp):
                for way in range(2):
                    for wave in range(WAVES):
                        parts, far = sums[wave]
                        part = parts[way]
                        if t > 1:
                            part = part + far[way][t - 2]
                        if t + 1 == n_grp and not final:
                            parts[way] = lax.ppermute(part, ("strat", "grp"), last[way])
                        else:
                            parts[way] = lax.ppermute(part, "grp", ring[way])
            got = [
                [[owns[wave][way] + sums[wave][0][way]] for way in range(2)]
                for wave in range(WAVES)
            ]
            for t in range(1, n_grp):
                for way in range(2):
                    for wave in range(WAVES):
                        tiles = got[wave][way]
                        tiles.append(lax.ppermute(tiles[-1], "grp", ring[way]))
            nexts = [tile for ways in got for tiles in ways for tile in tiles]
            users = after
            slabs = nexts
        items = None
        for wave in range(WAVES):
            tiles = slabs[2 * n_grp * wave : 2 * n_grp * (wave + 1)]
            items = lay(wave, n_grp, place, tiles, items)
        return users, items.reshape(item_factors.shape)

    placed = (
        P(("strat", "grp"), None),
        P("strat", None),
        P("strat", "grp", None, None, None),
        P("strat", "grp", None),
        P("strat", "grp", None, None, None, None),
    )
    return jax.shard_map(
        per_device,
        mesh=mesh,
        in_specs=placed,
        out_specs=(P(("strat", "grp"), None), P("strat", None)),
        check_vma=False,
    )
```
